32 devices in a mesh: groups: 2 (over y), blk: 8 (over z, x), heads: 2 (over core).
Axes of the slice: x: 2, y: 2, z: 4, core: 2. Of those that a mesh axis runs over, the one named last changes fastest.
Arguments:
- tokens: bfloat16 [6144, 1024], P(('groups', 'blk'), 'heads'), parts along dimension 0, may hold values from -96 to 96
- w_query: bfloat16 [1024, 1024], P(None, 'heads'), may hold values from -0.47851562 to 0.47851562
- w_key: bfloat16 [1024, 1024], P(None, 'heads'), may hold values from -0.1875 to 0.1875
- w_value: bfloat16 [1024, 1024], P(None, 'heads'), may hold values from -0.1875 to 0.1875
- hilbert_pos: int32 [6144], P(('groups', 'blk')), parts along dimension 0, may hold values from 0 to 3071, as said below
- key_blocks: int32 [48, 8], P(('groups', 'blk')), parts along dimension 0, may hold values from 0 to 23, as said below
- blend: int32 [6144], P(('groups', 'blk')), parts along dimension 0, may hold values from 1 to 8
Outputs:
- blended: bfloat16 [6144, 1024], P(('groups', 'blk'), 'heads'), parts along dimension 0
The draws below stay inside these ranges and needn't reach their ends.
There are 2 independent parts, one for each index of `groups`. The reference program is written for one: setup_inputs(seed, part) draws one part's arguments, and reference() takes and returns one part's arrays. A program takes and returns all parts, laid end to end along the dimension named above; an argument that names none is the same for every part. Nothing has to cross between parts.
Inputs may be any that keep to these rules, and one draw needn't show every extreme that they name: `hilbert_pos`: A permutation of the 3072 positions. Each index of blk holds the sequence positions i * 384 to (i + 1) * 384 - 1; the 384 tile tokens of each index of blk go to every index exactly 48 at a time. `key_blocks`: row b names 8 distinct blocks, b itself among them. Block c lies on index c // 3 of blk; every listed block lies at most 2 indices from b's along the closed cycle of blk, and some row names blocks exactly 2 indices below and above its own.
All inputs are finite; a program needn't handle non-finite values.
Results may differ from the reference program's by a relative error of at most 0.0025.
The reference program's roundings to bfloat16 on the way (of `ordered`, `rounded` and `attended`) count: a program that leaves them out, or rounds other values in their place, can miss the bound.
Values may be sent and summed in bfloat16 or wider, within the bound.
A program may use at most 64 MiB of HBM per device.

```python
import jax
import jax.numpy as jnp
from jax import lax

D = 1024
HEADS = 16
TOK_DEV = 384
BLOCK = 128
LIST = 8
REACH = 2
BLEND = 8
HEAD_DIM = 64
TOKENS = 3072
NBLOCKS = 24
N_BLK = 8


def shuffle_tokens(key_one):
    return jax.random.permutation(key_one, TOK_DEV).astype(jnp.int32)


def draw_hilbert_pos(key, part):
    key = jax.random.fold_in(key, 37)
    source_key, target_key = jax.random.split(key)
    per_peer = TOK_DEV // N_BLK
    local_order = jax.vmap(shuffle_tokens)(jax.random.split(source_key, N_BLK))
    slot_order = jax.vmap(shuffle_tokens)(jax.random.split(target_key, N_BLK))
    rank = jnp.arange(TOK_DEV, dtype=jnp.int32)
    owner = jnp.arange(N_BLK, dtype=jnp.int32)
    target = rank // per_peer
    incoming = owner[:, None] * per_peer + rank[None, :] % per_peer
    target_full = jnp.broadcast_to(target[None, :], (N_BLK, TOK_DEV))
    position = target_full * TOK_DEV + slot_order[target_full, incoming]
    token = owner[:, None] * TOK_DEV + local_order
    return jnp.zeros((TOKENS,), jnp.int32).at[token.reshape(-1)].set(position.reshape(-1).astype(jnp.int32))


def draw_key_blocks(key, part):
    key = jax.random.fold_in(key, 23)
    noise_key, force_key = jax.random.split(key)
    per_dev = TOK_DEV // BLOCK
    cands = (2 * REACH + 1) * per_dev
    noise = jax.random.randint(noise_key, (NBLOCKS, cands), 0, 2 ** 20)
    column = jnp.arange(cands, dtype=jnp.int32)
    row = jnp.arange(NBLOCKS, dtype=jnp.int32)
    own = REACH * per_dev + row % per_dev
    chosen = jax.random.randint(force_key, (), 0, NBLOCKS)
    ends = (column[None, :] == 0) | (column[None, :] == cands - 1)
    forced = (column[None, :] == own[:, None]) | (row[:, None] == chosen) & ends
    score = noise * 128 + column[None, :] + jnp.where(forced, 2 ** 28, 0)
    picked = lax.top_k(score, LIST)[1].astype(jnp.int32)
    home = row // per_dev
    device = (home[:, None] + picked // per_dev - REACH) % N_BLK
    return (device * per_dev + picked % per_dev).astype(jnp.int32)


def draw_tokens(key, part):
    key = jax.random.fold_in(key, 51)
    base_key = jax.random.fold_in(key, 0)
    values = jax.random.normal(base_key, (TOKENS, D), jnp.float32)
    values = jnp.clip(values, -6.0, 6.0)
    return values.astype(jnp.bfloat16)


def place_ends(values, key, least, top_value):
    place = [jax.random.randint(jax.random.fold_in(key, axis), (), 0, length) for axis, length in enumerate(values.shape)]
    widest = values.shape.index(max(values.shape))
    beside = place[:widest] + [(place[widest] + 1) % values.shape[widest]] + place[widest + 1:]
    return values.at[tuple(place)].set(least).at[tuple(beside)].set(top_value)


def block_levels(stream_key, extent, pieces, smallest, top_value):
    gain, own = 1.0, jax.random.fold_in(stream_key, 6)
    for axis_at, parts in pieces:
        steps = jnp.exp(jax.random.uniform(jax.random.fold_in(own, axis_at), (parts,), jnp.float32, smallest / len(pieces), top_value / len(pieces)))
        gain = gain * jnp.repeat(steps, extent[axis_at] // parts).reshape([-1 if axis == axis_at else 1 for axis in range(len(extent))])
    return gain


def bell_draw(key, extent, width, most, cuts=(), kind=jnp.bfloat16):
    result = width * jax.random.normal(key, extent, jnp.float32)
    if cuts:
        result = result * block_levels(key, extent, cuts, -0.22, 0.18)
    return jnp.clip(result, -most, most).astype(kind)


def setup_inputs(seed: int = 0, part: int = 0) -> dict:
    arg_keys = jax.random.split(jax.random.key(seed), 8)
    part_splits = jax.random.split(jax.random.fold_in(arg_keys[7], part), 8)
    return {
        "tokens": draw_tokens(jax.random.fold_in(jax.random.fold_in(arg_keys[7], part), 71), part),
        "w_query": bell_draw(arg_keys[1], (D, D), 0.08, 0.47851562, ((1, 2),)),
        "w_key": bell_draw(arg_keys[2], (D, D), D ** -0.5, 0.1875, ((1, 2),)),
        "w_value": bell_draw(arg_keys[3], (D, D), D ** -0.5, 0.1875, ((1, 2),)),
        "hilbert_pos": draw_hilbert_pos(jax.random.fold_in(jax.random.fold_in(arg_keys[7], part), 71), part),
        "key_blocks": draw_key_blocks(jax.random.fold_in(jax.random.fold_in(arg_keys[7], part), 71), part),
        "blend": place_ends(jax.random.randint(part_splits[6], (TOKENS,), 1, 9), jax.random.fold_in(part_splits[6], 1), 1, 8).astype(jnp.int32),
    }


def reference(tokens, w_query, w_key, w_value, hilbert_pos, key_blocks, blend):
    ordered = jnp.zeros_like(tokens).at[hilbert_pos].set(tokens)
    query = jnp.dot(ordered, w_query, preferred_element_type=jnp.float32).astype(jnp.bfloat16)
    keys = jnp.dot(ordered, w_key, preferred_element_type=jnp.float32).astype(jnp.bfloat16)
    values = jnp.dot(ordered, w_value, preferred_element_type=jnp.float32).astype(jnp.bfloat16)
    query_blocks = query.reshape(NBLOCKS, BLOCK, HEADS, HEAD_DIM)
    key_all = keys.reshape(NBLOCKS, BLOCK, HEADS, HEAD_DIM)
    value_all = values.reshape(NBLOCKS, BLOCK, HEADS, HEAD_DIM)

    def one_block(item):
        query_block, listed = item
        near_keys = key_all[listed].reshape(LIST * BLOCK, HEADS, HEAD_DIM)
        near_values = value_all[listed].reshape(LIST * BLOCK, HEADS, HEAD_DIM)
        scores = jnp.einsum("qhd,khd->hqk", query_block.astype(jnp.float32), near_keys.astype(jnp.float32)) * HEAD_DIM ** -0.5
        top = jnp.max(scores, axis=2, keepdims=True)
        weights = jnp.exp(scores - top)
        total = jnp.sum(weights, axis=2)
        rounded = weights.astype(jnp.bfloat16)
        mixed = jnp.einsum("hqk,khd->qhd", rounded.astype(jnp.float32), near_values.astype(jnp.float32))
        return (mixed / jnp.transpose(total)[:, :, None]).astype(jnp.bfloat16)

    attended = lax.map(one_block, (query_blocks, key_blocks)).reshape(TOKENS, D)
    back = attended[hilbert_pos]
    return (back.astype(jnp.float32) * blend.astype(jnp.float32)[:, None] / BLEND).astype(jnp.bfloat16)
```

```python
import functools

import jax
import jax.numpy as jnp
from jax import lax
from jax.experimental import pallas as pl
from jax.experimental.pallas import tpu as pltpu
from jax.sharding import PartitionSpec as P

BLOCK = 128
LIST = 8
REACH = 2
BLEND = 8
HEAD_DIM = 64
PIECES = 2
WINDOW = 2 * REACH + 1
LOG2_E = 1.4426950408889634
MESH = pl.DeviceIdType.MESH
F32 = jnp.float32
BF16 = jnp.bfloat16


def remote(src, dst, send_sem, recv_sem, where):
    return pltpu.make_async_remote_copy(
        src_ref=src,
        dst_ref=dst,
        send_sem=send_sem,
        recv_sem=recv_sem,
        device_id=where,
        device_id_type=MESH,
    )


def over_peers(n, body):
    if n <= 8:
        for k in range(1, n):
            body(k)
    else:
        lax.fori_loop(1, n, lambda k, c: (body(k), c)[1], 0)


def iota(shape, axis):
    return lax.broadcasted_iota(jnp.int32, shape, axis).astype(F32)


def contract(a, b, da, db):
    return lax.dot_general(a, b, (((da,), (db,)), ((), ())), preferred_element_type=F32)


def kernel(
    n, tok, pos, listed, wq, wk, wv, out,
    send, recv, code_out, code_in, spread, gather, win, qb, kb, vb, att, back_out, back_in, wq_v, wk_v, wv_v,
    w_sem, tok_s, tok_r, code_s, code_r, own_s, fwd_s, win_r, core_s, core_r, back_s, back_r,
):
    rows, width = tok.shape
    pp = send.shape[1]
    per_peer = rows // n
    nb = rows // BLOCK
    total_rows = n * pp
    me = lax.axis_index("blk")
    half = lax.axis_index("heads")
    e = 1 - 2 * lax.rem(me, 2)
    other = {"heads": 1 - half}

    def peer(k):
        return lax.rem(me + k + n, n)

    barrier = pltpu.get_barrier_semaphore()
    over_peers(n, lambda k: pl.semaphore_signal(barrier, inc=1, device_id={"blk": peer(k)}, device_id_type=MESH))
    pl.semaphore_signal(barrier, inc=1, device_id=other, device_id_type=MESH)

    loads = [
        pltpu.make_async_copy(src, dst, w_sem.at[i])
        for i, (src, dst) in enumerate(((wq, wq_v), (wk, wk_v), (wv, wv_v)))
    ]
    for load in loads:
        load.start()

    place = pos[...].astype(F32)
    column = jnp.sum(
        jnp.where(iota((rows, rows), 0) == iota((rows, rows), 1), place, 0.0), axis=1, keepdims=True
    )
    rank = jnp.sum(jnp.where(column < place, 1.0, 0.0), axis=0, keepdims=True)
    owner = jnp.sum(
        jnp.where(place >= (iota((n, rows), 0) + 1.0) * rows, 1.0, 0.0), axis=0, keepdims=True
    )
    slot_in = rank - owner * per_peer
    spread[...] = jnp.where(iota((total_rows, rows), 0) == owner * pp + slot_in, 1.0, 0.0).astype(BF16)
    code = place - owner * rows + 1.0
    high = jnp.floor(code * (1.0 / 128))
    low = code - high * 128
    mine = iota((n, rows), 0) == owner
    at = jnp.where(
        iota((total_rows, rows), 0) == slot_in + (me * pp).astype(F32), 1.0, 0.0
    ).astype(BF16)
    codes = 128.0 * contract(jnp.where(mine, high, 0.0).astype(BF16), at, 1, 1) + contract(
        jnp.where(mine, low, 0.0).astype(BF16), at, 1, 1
    )
    for d in range(n):
        code_out[d] = codes[d : d + 1, :]
    send[...] = contract(spread[...], tok[...], 1, 0).astype(BF16).reshape(n, pp, width)

    pl.semaphore_wait(barrier, n)

    def send_code(k):
        remote(code_out.at[peer(k)], code_in.at[me], code_s.at[k], code_r.at[k], {"blk": peer(k)}).start()

    def send_rows(k):
        remote(send.at[peer(k)], recv.at[me], tok_s.at[k], tok_r.at[k], {"blk": peer(k)}).start()

    over_peers(n, send_code)
    over_peers(n, send_rows)
    code_in[me] = code_out[me]
    recv[me] = send[me]

    def take_code(k):
        remote(code_out.at[peer(k)], code_in.at[peer(-k)], code_s.at[k], code_r.at[k], {"blk": peer(k)}).wait()

    def take_rows(k):
        remote(send.at[peer(k)], recv.at[peer(-k)], tok_s.at[k], tok_r.at[k], {"blk": peer(k)}).wait()

    over_peers(n, take_code)
    arrived = jnp.sum(code_in[...], axis=0)
    gather[...] = jnp.where(iota((rows, total_rows), 0) + 1.0 == arrived, 1.0, 0.0).astype(BF16)
    over_peers(n, take_rows)
    placed = contract(gather[...], recv[...].reshape(total_rows, width), 1, 0).astype(BF16)
    win[half, REACH] = placed

    def piece(step, c):
        return win.at[half, REACH + step, pl.ds(c * BLOCK, BLOCK)]

    def own_copy(i, step, c):
        return remote(
            piece(0, c), piece(-step, c), own_s.at[i, c], win_r.at[REACH - step, c], {"blk": peer(step)}
        )

    def fwd_copy(c):
        return remote(piece(2 * e, c), piece(e, c), fwd_s.at[c], win_r.at[REACH + e, c], {"blk": peer(e)})

    def core_copy(step, c):
        return remote(
            piece(step, c), piece(step, c), core_s.at[REACH + step, c], core_r.at[REACH + step, c], other
        )

    def arrival(step, c):
        return remote(piece(0, c), piece(step, c), own_s.at[0, c], win_r.at[REACH + step, c], {"blk": peer(step)})

    def core_arrival(step, c):
        return remote(
            piece(step, c),
            win.at[1 - half, REACH + step, pl.ds(c * BLOCK, BLOCK)],
            core_s.at[REACH + step, c],
            core_r.at[REACH + step, c],
            other,
        )

    steps_out = (-2 * e, 2 * e, e)
    for c in range(nb):
        for i, step in enumerate(steps_out):
            own_copy(i, step, c).start()
        core_copy(0, c).start()

    def project(step, with_query):
        for c in range(nb):
            core_arrival(step, c).wait_recv()
        slot = REACH + step
        whole = jnp.concatenate([win[0, slot], win[1, slot]], axis=1)
        if with_query:
            qb[...] = contract(whole, wq_v[...], 1, 0).astype(BF16).reshape(nb, BLOCK, width)
        kb[pl.ds(slot * nb, nb)] = contract(whole, wk_v[...], 1, 0).astype(BF16).reshape(nb, BLOCK, width)
        vb[pl.ds(slot * nb, nb)] = contract(whole, wv_v[...], 1, 0).astype(BF16).reshape(nb, BLOCK, width)

    def pass_on(step, forward):
        for c in range(nb):
            arrival(step, c).wait_recv()
            if forward:
                fwd_copy(c).start()
            core_copy(step, c).start()

    for load in loads:
        load.wait()
    project(0, True)
    pass_on(2 * e, True)
    pass_on(e, False)
    project(2 * e, False)
    project(e, False)
    pass_on(-2 * e, False)
    project(-2 * e, False)
    pass_on(-e, False)
    project(-e, False)

    first = lax.broadcasted_iota(jnp.int32, (BLOCK, 2 * HEAD_DIM), 1) < HEAD_DIM
    zero = jnp.zeros((BLOCK, 2 * HEAD_DIM), BF16)

    def attend(b, p, start):
        lanes = pl.ds(start, 2 * HEAD_DIM)
        slots = []
        for j in range(LIST):
            block = listed[b, j]
            away = jnp.minimum(lax.rem(lax.div(block, nb) - me + REACH + n, n), WINDOW - 1)
            slots.append(away * nb + lax.rem(block, nb))
        q = qb[b, :, lanes]
        both = jnp.concatenate([jnp.where(first, q, zero), jnp.where(first, zero, q)], axis=0)
        keys = jnp.concatenate([kb[s, :, lanes] for s in slots], axis=0)
        values = jnp.concatenate([vb[s, :, lanes] for s in slots], axis=0)
        scores = contract(both, keys, 1, 1)
        top = jnp.max(scores, axis=1, keepdims=True)
        weights = jnp.exp2((scores - top) * (HEAD_DIM ** (-0.5) * LOG2_E))
        total = jnp.sum(weights, axis=1, keepdims=True)
        mixed = contract(weights.astype(BF16), values, 1, 0) / total
        return jnp.where(first, mixed[:BLOCK], mixed[BLOCK:]).astype(BF16)

    part = width // PIECES
    pairs = part // (2 * HEAD_DIM)

    def back_copy(f, k, source):
        return remote(
            back_out.at[f, peer(k)], back_in.at[f, source], back_s.at[f, k], back_r.at[f, k], {"blk": peer(k)}
        )

    for f in range(PIECES):
        for p in range(pairs):

            @pl.loop(0, nb)
            def _(b):
                att[b, :, pl.ds(p * 2 * HEAD_DIM, 2 * HEAD_DIM)] = attend(b, p, f * part + p * 2 * HEAD_DIM)

        back_out[f] = (
            contract(gather[...], att[...].reshape(rows, part), 0, 0).astype(BF16).reshape(n, pp, part)
        )
        over_peers(n, lambda k: back_copy(f, k, me).start())
        back_in[f, me] = back_out[f, me]

    for c in range(nb):
        for i, step in enumerate(steps_out):
            own_copy(i, step, c).wait_send()
        fwd_copy(c).wait_send()
        for step in range(-REACH, REACH + 1):
            core_copy(step, c).wait_send()

    for f in range(PIECES):
        over_peers(n, lambda k: back_copy(f, k, peer(-k)).wait())
        out[:, pl.ds(f * part, part)] = contract(
            spread[...], back_in[f].reshape(total_rows, part), 0, 0
        ).astype(BF16)


def shards(n, tokens, w_query, w_key, w_value, hilbert_pos, key_blocks, blend):
    rows, width = tokens.shape
    depth = w_query.shape[0]
    per_peer = rows // n
    pp = -(-per_peer // 16) * 16
    nb = rows // BLOCK
    part = width // PIECES
    vmem = pl.BlockSpec(memory_space=pltpu.VMEM)
    anywhere = pl.BlockSpec(memory_space=pl.ANY)
    dma = pltpu.SemaphoreType.DMA
    restored = pl.pallas_call(
        functools.partial(kernel, n),
        out_shape=jax.ShapeDtypeStruct((rows, width), BF16),
        in_specs=[vmem, vmem, pl.BlockSpec(memory_space=pltpu.SMEM), anywhere, anywhere, anywhere],
        out_specs=vmem,
        scratch_shapes=[
            pltpu.VMEM((n, pp, width), BF16),
            pltpu.VMEM((n, pp, width), BF16),
            pltpu.VMEM((n, 1, n * pp), F32),
            pltpu.VMEM((n, 1, n * pp), F32),
            pltpu.VMEM((n * pp, rows), BF16),
            pltpu.VMEM((rows, n * pp), BF16),
            pltpu.VMEM((2, WINDOW, rows, width), BF16),
            pltpu.VMEM((nb, BLOCK, width), BF16),
            pltpu.VMEM((WINDOW * nb, BLOCK, width), BF16),
            pltpu.VMEM((WINDOW * nb, BLOCK, width), BF16),
            pltpu.VMEM((nb, BLOCK, part), BF16),
            pltpu.VMEM((PIECES, n, pp, part), BF16),
            pltpu.VMEM((PIECES, n, pp, part), BF16),
            pltpu.VMEM((depth, width), BF16),
            pltpu.VMEM((depth, width), BF16),
            pltpu.VMEM((depth, width), BF16),
            dma((3,)),
            dma((n,)),
            dma((n,)),
            dma((n,)),
            dma((n,)),
            dma((3, nb)),
            dma((nb,)),
            dma((WINDOW, nb)),
            dma((WINDOW, nb)),
            dma((WINDOW, nb)),
            dma((PIECES, n)),
            dma((PIECES, n)),
        ],
        compiler_params=pltpu.CompilerParams(
            collective_id=0, has_side_effects=True, vmem_limit_bytes=56 * 1024 * 1024
        ),
    )(tokens, hilbert_pos.reshape(1, rows), key_blocks, w_query, w_key, w_value)
    return (restored.astype(F32) * blend.astype(F32)[:, None] / BLEND).astype(BF16)


def solution(mesh):
    placed = (
        P(("groups", "blk"), "heads"),
        P(None, "heads"),
        P(None, "heads"),
        P(None, "heads"),
        P(("groups", "blk")),
        P(("groups", "blk"), None),
        P(("groups", "blk")),
    )
    return jax.shard_map(
        functools.partial(shards, mesh.shape["blk"]),
        mesh=mesh,
        in_specs=placed,
        out_specs=P(("groups", "blk"), "heads"),
        check_vma=False,
    )
```

```python
import functools

import jax
import jax.numpy as jnp
from jax import lax
from jax.experimental import pallas as pl
from jax.experimental.pallas import tpu as pltpu
from jax.sharding import PartitionSpec as P

BLOCK = 128
LIST = 8
REACH = 2
BLEND = 8
HEAD_DIM = 64
PIECES = 4
PARTS_IN = 2
WINDOW = 2 * REACH + 1
LOG2_E = 1.4426950408889634
MESH = pl.DeviceIdType.MESH
F32 = jnp.float32
BF16 = jnp.bfloat16


def remote(src, dst, send_sem, recv_sem, where):
    return pltpu.make_async_remote_copy(
        src_ref=src,
        dst_ref=dst,
        send_sem=send_sem,
        recv_sem=recv_sem,
        device_id=where,
        device_id_type=MESH,
    )


def over_peers(n, body):
    if n <= 8:
        for k in range(1, n):
            body(k)
    else:
        lax.fori_loop(1, n, lambda k, c: (body(k), c)[1], 0)


def iota(shape, axis):
    return lax.broadcasted_iota(jnp.int32, shape, axis).astype(F32)


def contract(a, b, da, db):
    return lax.dot_general(a, b, (((da,), (db,)), ((), ())), preferred_element_type=F32)


def kernel(
    n, tok, pos, blend, listed, wq, wk, wv, out,
    send, recv, code_out, code_in, spread, gather, scale, win, qb, kb, vb, att, back_out, back_in, wq_v, wk_v, wv_v,
    w_sem, tok_s, tok_r, code_s, code_r, own_s, fwd_s, win_r, core_s, core_r, back_s, back_r,
):
    rows, width = tok.shape
    pp = send.shape[2]
    piece_in = width // PARTS_IN
    per_peer = rows // n
    nb = rows // BLOCK
    total_rows = n * pp
    me = lax.axis_index("blk")
    half = lax.axis_index("heads")
    e = 1 - 2 * lax.rem(me, 2)
    other = {"heads": 1 - half}

    def peer(k):
        return lax.rem(me + k + n, n)

    barrier = pltpu.get_barrier_semaphore()
    over_peers(n, lambda k: pl.semaphore_signal(barrier, inc=1, device_id={"blk": peer(k)}, device_id_type=MESH))
    pl.semaphore_signal(barrier, inc=1, device_id=other, device_id_type=MESH)

    loads = [
        pltpu.make_async_copy(src, dst, w_sem.at[i])
        for i, (src, dst) in enumerate(((wq, wq_v), (wk, wk_v), (wv, wv_v)))
    ]
    for load in loads:
        load.start()

    place = pos[...].reshape(1, rows).astype(F32)
    diagonal = iota((rows, rows), 0) == iota((rows, rows), 1)

    def stand(row):
        return jnp.sum(jnp.where(diagonal, row, 0.0), axis=1, keepdims=True)

    column = stand(place)
    scale[...] = stand(blend[...].reshape(1, rows).astype(F32))
    rank = jnp.sum(jnp.where(column < place, 1.0, 0.0), axis=0, keepdims=True)
    owner = jnp.sum(
        jnp.where(place >= (iota((n, rows), 0) + 1.0) * rows, 1.0, 0.0), axis=0, keepdims=True
    )
    slot_in = rank - owner * per_peer
    spread[...] = jnp.where(iota((total_rows, rows), 0) == owner * pp + slot_in, 1.0, 0.0).astype(BF16)
    code = place - owner * rows + 1.0
    high = jnp.floor(code * (1.0 / 128))
    low = code - high * 128
    mine = iota((n, rows), 0) == owner
    at = jnp.where(
        iota((total_rows, rows), 0) == slot_in + (me * pp).astype(F32), 1.0, 0.0
    ).astype(BF16)
    codes = 128.0 * contract(jnp.where(mine, high, 0.0).astype(BF16), at, 1, 1) + contract(
        jnp.where(mine, low, 0.0).astype(BF16), at, 1, 1
    )
    for d in range(n):
        code_out[d] = codes[d : d + 1, :]
    for f in range(PARTS_IN):
        send[f] = (
            contract(spread[...], tok[:, pl.ds(f * piece_in, piece_in)], 1, 0)
            .astype(BF16)
            .reshape(n, pp, piece_in)
        )

    pl.semaphore_wait(barrier, n)

    def send_code(k):
        remote(code_out.at[peer(k)], code_in.at[me], code_s.at[k], code_r.at[k], {"blk": peer(k)}).start()

    def rows_copy(f, k, source):
        return remote(send.at[f, peer(k)], recv.at[f, source], tok_s.at[f, k], tok_r.at[f, k], {"blk": peer(k)})

    over_peers(n, send_code)
    for f in range(PARTS_IN):
        over_peers(n, lambda k: rows_copy(f, k, me).start())
        recv[f, me] = send[f, me]
    code_in[me] = code_out[me]

    def take_code(k):
        remote(code_out.at[peer(k)], code_in.at[peer(-k)], code_s.at[k], code_r.at[k], {"blk": peer(k)}).wait()

    over_peers(n, take_code)
    arrived = jnp.sum(code_in[...], axis=0)
    gather[...] = jnp.where(iota((rows, total_rows), 0) + 1.0 == arrived, 1.0, 0.0).astype(BF16)

    def piece(step, c):
        return win.at[half * PARTS_IN + c, REACH + step]

    def own_copy(i, step, c):
        return remote(
            piece(0, c), piece(-step, c), own_s.at[i, c], win_r.at[REACH - step, c], {"blk": peer(step)}
        )

    def fwd_copy(c):
        return remote(piece(2 * e, c), piece(e, c), fwd_s.at[c], win_r.at[REACH + e, c], {"blk": peer(e)})

    def core_copy(step, c):
        return remote(
            piece(step, c), piece(step, c), core_s.at[REACH + step, c], core_r.at[REACH + step, c], other
        )

    def arrival(step, c):
        return remote(piece(0, c), piece(step, c), own_s.at[0, c], win_r.at[REACH + step, c], {"blk": peer(step)})

    def core_arrival(step, c):
        return remote(
            piece(step, c),
            win.at[(1 - half) * PARTS_IN + c, REACH + step],
            core_s.at[REACH + step, c],
            core_r.at[REACH + step, c],
            other,
        )

    steps_out = (-2 * e, 2 * e, e)
    for c in range(PARTS_IN):
        over_peers(n, lambda k: rows_copy(c, k, peer(-k)).wait())
        win[half * PARTS_IN + c, REACH] = contract(
            gather[...], recv[c].reshape(total_rows, piece_in), 1, 0
        ).astype(BF16)
        own_copy(0, steps_out[0], c).start()
        core_copy(0, c).start()
        for i in (1, 2):
            own_copy(i, steps_out[i], c).start()

    def project(step, with_query):
        for c in range(PARTS_IN):
            core_arrival(step, c).wait_recv()
        slot = REACH + step
        whole = jnp.concatenate([win[g, slot] for g in range(2 * PARTS_IN)], axis=1)
        if with_query:
            qb[...] = contract(whole, wq_v[...], 1, 0).astype(BF16).reshape(nb, BLOCK, width)
        kb[pl.ds(slot * nb, nb)] = contract(whole, wk_v[...], 1, 0).astype(BF16).reshape(nb, BLOCK, width)
        vb[pl.ds(slot * nb, nb)] = contract(whole, wv_v[...], 1, 0).astype(BF16).reshape(nb, BLOCK, width)

    def pass_on(step, forward):
        for c in range(PARTS_IN):
            arrival(step, c).wait_recv()
            if forward:
                fwd_copy(c).start()
            core_copy(step, c).start()

    for load in loads:
        load.wait()
    project(0, True)
    pass_on(2 * e, True)
    pass_on(e, False)
    project(2 * e, False)
    project(e, False)
    pass_on(-2 * e, False)
    project(-2 * e, False)
    pass_on(-e, False)
    project(-e, False)

    first = lax.broadcasted_iota(jnp.int32, (BLOCK, 2 * HEAD_DIM), 1) < HEAD_DIM
    zero = jnp.zeros((BLOCK, 2 * HEAD_DIM), BF16)

    def attend(b, p, start):
        lanes = pl.ds(start, 2 * HEAD_DIM)
        slots = []
        for j in range(LIST):
            block = listed[b, j]
            away = jnp.minimum(lax.rem(lax.div(block, nb) - me + REACH + n, n), WINDOW - 1)
            slots.append(away * nb + lax.rem(block, nb))
        q = qb[b, :, lanes]
        both = jnp.concatenate([jnp.where(first, q, zero), jnp.where(first, zero, q)], axis=0)
        keys = jnp.concatenate([kb[s, :, lanes] for s in slots], axis=0)
        values = jnp.concatenate([vb[s, :, lanes] for s in slots], axis=0)
        scores = contract(both, keys, 1, 1)
        top = jnp.max(scores, axis=1, keepdims=True)
        weights = jnp.exp2((scores - top) * (HEAD_DIM ** (-0.5) * LOG2_E))
        total = jnp.sum(weights, axis=1, keepdims=True)
        mixed = contract(weights.astype(BF16), values, 1, 0) / total
        return jnp.where(first, mixed[:BLOCK], mixed[BLOCK:]).astype(BF16)

    part = width // PIECES
    pairs = part // (2 * HEAD_DIM)

    def back_copy(f, k, source):
        return remote(
            back_out.at[f, peer(k)], back_in.at[f, source], back_s.at[f, k], back_r.at[f, k], {"blk": peer(k)}
        )

    for f in range(PIECES):
        for p in range(pairs):
            for b in range(nb):
                att[b, :, pl.ds(p * 2 * HEAD_DIM, 2 * HEAD_DIM)] = attend(b, p, f * part + p * 2 * HEAD_DIM)

        back_out[f] = (
            contract(gather[...], att[...].reshape(rows, part), 0, 0).astype(BF16).reshape(n, pp, part)
        )
        over_peers(n, lambda k: back_copy(f, k, me).start())
        back_in[f, me] = back_out[f, me]

    for c in range(PARTS_IN):
        for i, step in enumerate(steps_out):
            own_copy(i, step, c).wait_send()
        fwd_copy(c).wait_send()
        for step in range(-REACH, REACH + 1):
            core_copy(step, c).wait_send()

    for f in range(PIECES):
        over_peers(n, lambda k: back_copy(f, k, peer(-k)).wait())
        restored = contract(spread[...], back_in[f].reshape(total_rows, part), 0, 0)
        out[:, pl.ds(f * part, part)] = (restored * scale[...] * (1.0 / BLEND)).astype(BF16)


def shards(n, tokens, w_query, w_key, w_value, hilbert_pos, key_blocks, blend):
    rows, width = tokens.shape
    depth = w_query.shape[0]
    per_peer = rows // n
    pp = -(-per_peer // 16) * 16
    nb = rows // BLOCK
    part = width // PIECES
    vmem = pl.BlockSpec(memory_space=pltpu.VMEM)
    anywhere = pl.BlockSpec(memory_space=pl.ANY)
    dma = pltpu.SemaphoreType.DMA
    return pl.pallas_call(
        functools.partial(kernel, n),
        out_shape=jax.ShapeDtypeStruct((rows, width), BF16),
        in_specs=[vmem, vmem, vmem, pl.BlockSpec(memory_space=pltpu.SMEM), anywhere, anywhere, anywhere],
        out_specs=vmem,
        scratch_shapes=[
            pltpu.VMEM((PARTS_IN, n, pp, width // PARTS_IN), BF16),
            pltpu.VMEM((PARTS_IN, n, pp, width // PARTS_IN), BF16),
            pltpu.VMEM((n, 1, n * pp), F32),
            pltpu.VMEM((n, 1, n * pp), F32),
            pltpu.VMEM((n * pp, rows), BF16),
            pltpu.VMEM((rows, n * pp), BF16),
            pltpu.VMEM((rows, 1), F32),
            pltpu.VMEM((2 * PARTS_IN, WINDOW, rows, width // PARTS_IN), BF16),
            pltpu.VMEM((nb, BLOCK, width), BF16),
            pltpu.VMEM((WINDOW * nb, BLOCK, width), BF16),
            pltpu.VMEM((WINDOW * nb, BLOCK, width), BF16),
            pltpu.VMEM((nb, BLOCK, part), BF16),
            pltpu.VMEM((PIECES, n, pp, part), BF16),
            pltpu.VMEM((PIECES, n, pp, part), BF16),
            pltpu.VMEM((depth, width), BF16),
            pltpu.VMEM((depth, width), BF16),
            pltpu.VMEM((depth, width), BF16),
            dma((3,)),
            dma((PARTS_IN, n)),
            dma((PARTS_IN, n)),
            dma((n,)),
            dma((n,)),
            dma((3, PARTS_IN)),
            dma((PARTS_IN,)),
            dma((WINDOW, PARTS_IN)),
            dma((WINDOW, PARTS_IN)),
            dma((WINDOW, PARTS_IN)),
            dma((PIECES, n)),
            dma((PIECES, n)),
        ],
        compiler_params=pltpu.CompilerParams(
            collective_id=0, has_side_effects=True, vmem_limit_bytes=56 * 1024 * 1024
        ),
    )(tokens, hilbert_pos, blend, key_blocks, w_query, w_key, w_value)


def solution(mesh):
    placed = (
        P(("groups", "blk"), "heads"),
        P(None, "heads"),
        P(None, "heads"),
        P(None, "heads"),
        P(("groups", "blk")),
        P(("groups", "blk"), None),
        P(("groups", "blk")),
    )
    return jax.shard_map(
        functools.partial(shards, mesh.shape["blk"]),
        mesh=mesh,
        in_specs=placed,
        out_specs=P(("groups", "blk"), "heads"),
        check_vma=False,
    )
```

```python
import functools

import jax
import jax.numpy as jnp
from jax import lax
from jax.experimental import pallas as pl
from jax.experimental.pallas import tpu as pltpu
from jax.sharding import PartitionSpec as P

BLOCK = 128
LIST = 8
REACH = 2
BLEND = 8
HEAD_DIM = 64
PIECES = 4
PARTS_IN = 2
WINDOW = 2 * REACH + 1
LOG2_E = 1.4426950408889634
MESH = pl.DeviceIdType.MESH
F32 = jnp.float32
BF16 = jnp.bfloat16


def remote(src, dst, send_sem, recv_sem, where):
    return pltpu.make_async_remote_copy(
        src_ref=src,
        dst_ref=dst,
        send_sem=send_sem,
        recv_sem=recv_sem,
        device_id=where,
        device_id_type=MESH,
    )


def over_peers(n, body):
    if n <= 8:
        for k in range(1, n):
            body(k)
    else:
        lax.fori_loop(1, n, lambda k, c: (body(k), c)[1], 0)


def iota(shape, axis):
    return lax.broadcasted_iota(jnp.int32, shape, axis).astype(F32)


def contract(a, b, da, db):
    return lax.dot_general(a, b, (((da,), (db,)), ((), ())), preferred_element_type=F32)


def kernel(
    n, tok, pos, blend, listed, wq, wk, wv, out,
    send, recv, code_out, code_in, spread, gather, scale, win, qb, kb, vb, att, back_out, back_in, wq_v, wk_v, wv_v,
    w_sem, tok_s, tok_r, code_s, code_r, own_s, fwd_s, win_r, core_s, core_r, back_s, back_r,
):
    rows, width = tok.shape
    pp = send.shape[2]
    piece_in = width // PARTS_IN
    per_peer = rows // n
    nb = rows // BLOCK
    total_rows = n * pp
    me = lax.axis_index("blk")
    half = lax.axis_index("heads")
    e = 1 - 2 * lax.rem(me, 2)
    other = {"heads": 1 - half}

    def peer(k):
        return lax.rem(me + k + n, n)

    barrier = pltpu.get_barrier_semaphore()
    over_peers(n, lambda k: pl.semaphore_signal(barrier, inc=1, device_id={"blk": peer(k)}, device_id_type=MESH))
    pl.semaphore_signal(barrier, inc=1, device_id=other, device_id_type=MESH)

    loads = [
        pltpu.make_async_copy(src, dst, w_sem.at[i])
        for i, (src, dst) in enumerate(((wq, wq_v), (wk, wk_v), (wv, wv_v)))
    ]
    for load in loads:
        load.start()

    place = pos[...].reshape(1, rows).astype(F32)
    diagonal = iota((rows, rows), 0) == iota((rows, rows), 1)

    def stand(row):
        return jnp.sum(jnp.where(diagonal, row, 0.0), axis=1, keepdims=True)

    column = stand(place)
    scale[...] = stand(blend[...].reshape(1, rows).astype(F32))
    rank = jnp.sum(jnp.where(column < place, 1.0, 0.0), axis=0, keepdims=True)
    owner = jnp.sum(
        jnp.where(place >= (iota((n, rows), 0) + 1.0) * rows, 1.0, 0.0), axis=0, keepdims=True
    )
    slot_in = rank - owner * per_peer
    spread[...] = jnp.where(iota((total_rows, rows), 0) == owner * pp + slot_in, 1.0, 0.0).astype(BF16)
    code = place - owner * rows + 1.0
    high = jnp.floor(code * (1.0 / 128))
    low = code - high * 128
    mine = iota((n, rows), 0) == owner
    at = jnp.where(
        iota((total_rows, rows), 0) == slot_in + (me * pp).astype(F32), 1.0, 0.0
    ).astype(BF16)
    codes = 128.0 * contract(jnp.where(mine, high, 0.0).astype(BF16), at, 1, 1) + contract(
        jnp.where(mine, low, 0.0).astype(BF16), at, 1, 1
    )
    for d in range(n):
        code_out[d] = codes[d : d + 1, :]
    for f in range(PARTS_IN):
        send[f] = (
            contract(spread[...], tok[:, pl.ds(f * piece_in, piece_in)], 1, 0)
            .astype(BF16)
            .reshape(n, pp, piece_in)
        )

    pl.semaphore_wait(barrier, n)

    def send_code(k):
        remote(code_out.at[peer(k)], code_in.at[me], code_s.at[k], code_r.at[k], {"blk": peer(k)}).start()

    def rows_copy(f, k, source):
        return remote(send.at[f, peer(k)], recv.at[f, source], tok_s.at[f, k], tok_r.at[f, k], {"blk": peer(k)})

    over_peers(n, send_code)
    for f in range(PARTS_IN):
        over_peers(n, lambda k: rows_copy(f, k, me).start())
        recv[f, me] = send[f, me]
    code_in[me] = code_out[me]

    def take_code(k):
        remote(code_out.at[peer(k)], code_in.at[peer(-k)], code_s.at[k], code_r.at[k], {"blk": peer(k)}).wait()

    over_peers(n, take_code)
    arrived = jnp.sum(code_in[...], axis=0)
    gather[...] = jnp.where(iota((rows, total_rows), 0) + 1.0 == arrived, 1.0, 0.0).astype(BF16)

    def piece(step, c):
        return win.at[half * PARTS_IN + c, REACH + step]

    def own_copy(i, step, c):
        return remote(
            piece(0, c), piece(-step, c), own_s.at[i, c], win_r.at[REACH - step, c], {"blk": peer(step)}
        )

    def fwd_copy(c):
        return remote(piece(2 * e, c), piece(e, c), fwd_s.at[c], win_r.at[REACH + e, c], {"blk": peer(e)})

    def core_copy(step, c):
        return remote(
            piece(step, c), piece(step, c), core_s.at[REACH + step, c], core_r.at[REACH + step, c], other
        )

    def arrival(step, c):
        return remote(piece(0, c), piece(step, c), own_s.at[0, c], win_r.at[REACH + step, c], {"blk": peer(step)})

    def core_arrival(step, c):
        return remote(
            piece(step, c),
            win.at[(1 - half) * PARTS_IN + c, REACH + step],
            core_s.at[REACH + step, c],
            core_r.at[REACH + step, c],
            other,
        )

    steps_out = (-2 * e, 2 * e, e)
    for c in range(PARTS_IN):
        over_peers(n, lambda k: rows_copy(c, k, peer(-k)).wait())
        win[half * PARTS_IN + c, REACH] = contract(
            gather[...], recv[c].reshape(total_rows, piece_in), 1, 0
        ).astype(BF16)
        own_copy(0, steps_out[0], c).start()
        core_copy(0, c).start()
        for i in (1, 2):
            own_copy(i, steps_out[i], c).start()

    def project(step, with_query):
        for c in range(PARTS_IN):
            core_arrival(step, c).wait_recv()
        slot = REACH + step
        whole = jnp.concatenate([win[g, slot] for g in range(2 * PARTS_IN)], axis=1)
        if with_query:
            qb[...] = contract(whole, wq_v[...], 1, 0).astype(BF16).reshape(nb, BLOCK, width)
        kb[pl.ds(slot * nb, nb)] = contract(whole, wk_v[...], 1, 0).astype(BF16).reshape(nb, BLOCK, width)
        vb[pl.ds(slot * nb, nb)] = contract(whole, wv_v[...], 1, 0).astype(BF16).reshape(nb, BLOCK, width)

    def pass_on(step, forward):
        for c in range(PARTS_IN):
            arrival(step, c).wait_recv()
            if forward:
                fwd_copy(c).start()
            core_copy(step, c).start()

    for load in loads:
        load.wait()
    project(0, True)
    pass_on(2 * e, True)
    pass_on(e, False)
    project(2 * e, False)
    project(e, False)
    pass_on(-2 * e, False)
    pass_on(-e, False)
    project(-2 * e, False)
    project(-e, False)

    first = lax.broadcasted_iota(jnp.int32, (BLOCK, 2 * HEAD_DIM), 1) < HEAD_DIM
    zero = jnp.zeros((BLOCK, 2 * HEAD_DIM), BF16)

    def attend(b, p, start):
        lanes = pl.ds(start, 2 * HEAD_DIM)
        slots = []
        for j in range(LIST):
            block = listed[b, j]
            away = jnp.minimum(lax.rem(lax.div(block, nb) - me + REACH + n, n), WINDOW - 1)
            slots.append(away * nb + lax.rem(block, nb))
        q = qb[b, :, lanes]
        both = jnp.concatenate([jnp.where(first, q, zero), jnp.where(first, zero, q)], axis=0)
        keys = jnp.concatenate([kb[s, :, lanes] for s in slots], axis=0)
        values = jnp.concatenate([vb[s, :, lanes] for s in slots], axis=0)
        scores = contract(both, keys, 1, 1)
        top = jnp.max(scores, axis=1, keepdims=True)
        weights = jnp.exp2((scores - top) * (HEAD_DIM ** (-0.5) * LOG2_E))
        total = jnp.sum(weights, axis=1, keepdims=True)
        mixed = contract(weights.astype(BF16), values, 1, 0) / total
        return jnp.where(first, mixed[:BLOCK], mixed[BLOCK:]).astype(BF16)

    part = width // PIECES
    pairs = part // (2 * HEAD_DIM)

    def back_copy(f, k, source):
        return remote(
            back_out.at[f, peer(k)], back_in.at[f, source], back_s.at[f, k], back_r.at[f, k], {"blk": peer(k)}
        )

    for f in range(PIECES):
        for p in range(pairs):
            for b in range(nb):
                att[b, :, pl.ds(p * 2 * HEAD_DIM, 2 * HEAD_DIM)] = attend(b, p, f * part + p * 2 * HEAD_DIM)

        back_out[f] = (
            contract(gather[...], att[...].reshape(rows, part), 0, 0).astype(BF16).reshape(n, pp, part)
        )
        over_peers(n, lambda k: back_copy(f, k, me).start())
        back_in[f, me] = back_out[f, me]

    for c in range(PARTS_IN):
        for i, step in enumerate(steps_out):
            own_copy(i, step, c).wait_send()
        fwd_copy(c).wait_send()
        for step in range(-REACH, REACH + 1):
            core_copy(step, c).wait_send()

    for f in range(PIECES):
        over_peers(n, lambda k: back_copy(f, k, peer(-k)).wait())
        restored = contract(spread[...], back_in[f].reshape(total_rows, part), 0, 0)
        out[:, pl.ds(f * part, part)] = (restored * scale[...] * (1.0 / BLEND)).astype(BF16)


def shards(n, tokens, w_query, w_key, w_value, hilbert_pos, key_blocks, blend):
    rows, width = tokens.shape
    depth = w_query.shape[0]
    per_peer = rows // n
    pp = -(-per_peer // 16) * 16
    nb = rows // BLOCK
    part = width // PIECES
    vmem = pl.BlockSpec(memory_space=pltpu.VMEM)
    anywhere = pl.BlockSpec(memory_space=pl.ANY)
    dma = pltpu.SemaphoreType.DMA
    return pl.pallas_call(
        functools.partial(kernel, n),
        out_shape=jax.ShapeDtypeStruct((rows, width), BF16),
        in_specs=[vmem, vmem, vmem, pl.BlockSpec(memory_space=pltpu.SMEM), anywhere, anywhere, anywhere],
        out_specs=vmem,
        scratch_shapes=[
            pltpu.VMEM((PARTS_IN, n, pp, width // PARTS_IN), BF16),
            pltpu.VMEM((PARTS_IN, n, pp, width // PARTS_IN), BF16),
            pltpu.VMEM((n, 1, n * pp), F32),
            pltpu.VMEM((n, 1, n * pp), F32),
            pltpu.VMEM((n * pp, rows), BF16),
            pltpu.VMEM((rows, n * pp), BF16),
            pltpu.VMEM((rows, 1), F32),
            pltpu.VMEM((2 * PARTS_IN, WINDOW, rows, width // PARTS_IN), BF16),
            pltpu.VMEM((nb, BLOCK, width), BF16),
            pltpu.VMEM((WINDOW * nb, BLOCK, width), BF16),
            pltpu.VMEM((WINDOW * nb, BLOCK, width), BF16),
            pltpu.VMEM((nb, BLOCK, part), BF16),
            pltpu.VMEM((PIECES, n, pp, part), BF16),
            pltpu.VMEM((PIECES, n, pp, part), BF16),
            pltpu.VMEM((depth, width), BF16),
            pltpu.VMEM((depth, width), BF16),
            pltpu.VMEM((depth, width), BF16),
            dma((3,)),
            dma((PARTS_IN, n)),
            dma((PARTS_IN, n)),
            dma((n,)),
            dma((n,)),
            dma((3, PARTS_IN)),
            dma((PARTS_IN,)),
            dma((WINDOW, PARTS_IN)),
            dma((WINDOW, PARTS_IN)),
            dma((WINDOW, PARTS_IN)),
            dma((PIECES, n)),
            dma((PIECES, n)),
        ],
        compiler_params=pltpu.CompilerParams(
            collective_id=0, has_side_effects=True, vmem_limit_bytes=56 * 1024 * 1024
        ),
    )(tokens, hilbert_pos, blend, key_blocks, w_query, w_key, w_value)


def solution(mesh):
    placed = (
        P(("groups", "blk"), "heads"),
        P(None, "heads"),
        P(None, "heads"),
        P(None, "heads"),
        P(("groups", "blk")),
        P(("groups", "blk"), None),
        P(("groups", "blk")),
    )
    return jax.shard_map(
        functools.partial(shards, mesh.shape["blk"]),
        mesh=mesh,
        in_specs=placed,
        out_specs=P(("groups", "blk"), "heads"),
        check_vma=False,
    )
```
